32 devices in a mesh: groups: 2 (over x), tile: 16 (over z, y, core).
Axes of the slice: x: 2, y: 2, z: 4, core: 2. Of those that a mesh axis runs over, the one named last changes fastest.
Arguments:
- ref_feat: bfloat16 [64, 256, 256], P('groups', 'tile'), parts along dimension 0, may hold values from -6 to 6
- src_feat: bfloat16 [8, 32, 256, 256], P('groups', None, 'tile'), parts along dimension 0, may hold values from -6 to 6
- row_tap: int32 [8, 32, 256], P('groups', None, 'tile'), parts along dimension 0, may hold values from 0 to 254, as said below
- row_frac: bfloat16 [8, 32, 256], P('groups', None, 'tile'), parts along dimension 0, may hold values from 0 to 1
- col_tap: int32 [8, 32, 256], P('groups'), parts along dimension 0, may hold values from 0 to 254
- col_frac: bfloat16 [8, 32, 256], P('groups'), parts along dimension 0, may hold values from 0 to 1
- view_count: int32 [32], P(('groups', 'tile')), parts along dimension 0, may hold values from 1 to 4
- conv_weight: bfloat16 [3, 3, 3, 8, 32], replicated, may hold values from -0.21875 to 0.21875
- conv_bias: float32 [8], replicated, may hold values from -1 to 1
Outputs:
- cost_volume: bfloat16 [64, 8, 256, 256], P('groups', None, 'tile'), parts along dimension 0
The draws below stay inside these ranges and needn't reach their ends.
There are 2 independent parts, one for each index of `groups`. The reference program is written for one: setup_inputs(seed, part) draws one part's arguments, and reference() takes and returns one part's arrays. A program takes and returns all parts, laid end to end along the dimension named above; an argument that names none is the same for every part. Nothing has to cross between parts.
Inputs may be any that keep to these rules, and one draw needn't show every extreme that they name: For reference rows of strip t (rows t * 16 to (t + 1) * 16 - 1), row_tap and row_tap + 1 lie in rows max(0, (t - 2) * 16) to min(256, (t + 3) * 16) - 1.
All inputs are finite; a program needn't handle non-finite values.
Results may differ from the reference program's by a relative error of at most 0.0051.
Values may be sent and summed in bfloat16 or wider, within the bound.
No kernel may reach another device: no remote copies, remote signals or barrier semaphores. Data moves between devices by JAX's collectives and lax.ppermute only.
A program may use at most 192 MiB of HBM per device.

```python
import jax
import jax.numpy as jnp
from jax import lax

C = 32
OUTC = 8
PLANES = 32
SRC = 4
REACH = 2
ROWS = 16
COLS = 256
TILES = 16
HEIGHT = 256


def draw_row_tap(key, part):
    key = jax.random.fold_in(key, 11)
    first_key, second_key = jax.random.split(key)
    offsets = jax.random.randint(first_key, (SRC, PLANES, TILES), -REACH * ROWS, REACH * ROWS + 1)
    offsets = offsets.at[0, 0, :].set(-REACH * ROWS).at[0, PLANES - 1, :].set(REACH * ROWS)
    jitter = jax.random.randint(second_key, (SRC, PLANES, HEIGHT), -1, 2)
    positions = jnp.arange(HEIGHT)
    owner = positions // ROWS
    taps = positions[None, None, :] + offsets[:, :, owner] + jitter
    lowest = jnp.maximum((owner - REACH) * ROWS, 0)
    highest = jnp.minimum((owner + REACH + 1) * ROWS, HEIGHT) - 2
    return jnp.clip(taps, lowest[None, None, :], highest[None, None, :]).astype(jnp.int32)


def draw_col_tap(key, part):
    key = jax.random.fold_in(key, 12)
    first_key, second_key = jax.random.split(key)
    offsets = jax.random.randint(first_key, (SRC, PLANES, 1), -(COLS // 8), COLS // 8 + 1)
    offsets = offsets.at[0, 0, 0].set(-(COLS // 8))
    jitter = jax.random.randint(second_key, (SRC, PLANES, COLS), -2, 3)
    positions = jnp.arange(COLS)
    taps = positions[None, None, :] + offsets + jitter
    return jnp.clip(taps, 0, COLS - 2).astype(jnp.int32)


def draw_view_count(key, part):
    key = jax.random.fold_in(key, 13)
    first_key, second_key = jax.random.split(key)
    counts = jax.random.randint(first_key, (TILES,), 1, SRC + 1)
    chosen = jax.random.randint(second_key, (), 0, TILES)
    counts = counts.at[chosen].set(SRC).at[(chosen + 1) % TILES].set(1)
    return counts.astype(jnp.int32)


def block_scale(stream_key, extent, cuts, smallest, top_value):
    gain = 1.0
    for axis_at, shards_of in cuts:
        heights = jax.random.uniform(jax.random.fold_in(jax.random.fold_in(stream_key, 6), axis_at), (shards_of,), jnp.float32, smallest / len(cuts), top_value / len(cuts))
        gain = gain * jnp.repeat(jnp.exp(heights), extent[axis_at] // shards_of).reshape((-1,) + (1,) * (len(extent) - 1 - axis_at))
    return gain


def bell_draw(stream_key, extent, scale, most, pieces=(), kind=jnp.bfloat16):
    factor_of = block_scale(stream_key, extent, pieces, -0.22, 0.18) if pieces else 1.0
    drawn = jax.random.normal(stream_key, extent, jnp.float32) * scale * factor_of
    return jnp.minimum(jnp.maximum(drawn, -most), most).astype(kind)


def setup_inputs(seed: int = 0, part: int = 0) -> dict:
    seeds = jax.random.split(jax.random.key(seed), 10)
    own_keys = jax.random.split(jax.random.fold_in(seeds[9], part), 10)
    ref_feat = bell_draw(own_keys[0], (C, HEIGHT, COLS), 1.0, 6.0, ((1, 16),))
    src_feat = bell_draw(own_keys[1], (SRC, C, HEIGHT, COLS), 1.0, 6.0, ((2, 16),))
    row_tap = draw_row_tap(jax.random.fold_in(jax.random.fold_in(seeds[9], part), 71), part)
    row_frac = jnp.clip(1.0 * jax.random.uniform(own_keys[3], (SRC, PLANES, HEIGHT), jnp.float32) ** block_scale(own_keys[3], (SRC, PLANES, HEIGHT), ((2, 16),), -0.2, 0.2), 0.0, 1.0).astype(jnp.bfloat16)
    col_tap = draw_col_tap(jax.random.fold_in(jax.random.fold_in(seeds[9], part), 71), part)
    col_frac = jnp.clip(jax.random.uniform(own_keys[5], (SRC, PLANES, COLS), jnp.float32, 0.0, 1.0), 0.0, 1.0).astype(jnp.bfloat16)
    view_count = draw_view_count(jax.random.fold_in(jax.random.fold_in(seeds[9], part), 71), part)
    conv_weight = bell_draw(seeds[7], (3, 3, 3, OUTC, C), (27 * C) ** -0.5, 0.21875)
    conv_bias = jnp.clip(jax.random.uniform(seeds[8], (OUTC,), jnp.float32, -1.0, 1.0), -1.0, 1.0)
    return {"ref_feat": ref_feat, "src_feat": src_feat, "row_tap": row_tap, "row_frac": row_frac, "col_tap": col_tap, "col_frac": col_frac, "view_count": view_count, "conv_weight": conv_weight, "conv_bias": conv_bias}


def stacked_columns(plane):
    width = plane.shape[2]
    padded = jnp.pad(plane, ((0, 0), (0, 0), (1, 1)))
    return jnp.concatenate([padded[:, :, 0:width], padded[:, :, 1:width + 1], padded[:, :, 2:width + 2]], axis=0)


def row_term(trio, weight_mats, offset):
    total = jnp.einsum('oc,crw->orw', weight_mats[0, offset].astype(jnp.float32), trio[0].astype(jnp.float32))
    for depth_tap in range(1, 3):
        total = total + jnp.einsum('oc,crw->orw', weight_mats[depth_tap, offset].astype(jnp.float32), trio[depth_tap].astype(jnp.float32))
    return total


def reference(ref_feat, src_feat, row_tap, row_frac, col_tap, col_frac, view_count, conv_weight, conv_bias):
    weight_mats = jnp.transpose(conv_weight, (0, 1, 3, 2, 4)).reshape(3, 3, OUTC, 3 * C)
    counts_rows = jnp.repeat(view_count, ROWS)
    valid = (jnp.arange(SRC)[:, None] < counts_rows[None, :]).astype(jnp.float32)
    divisor = 1.0 + counts_rows.astype(jnp.float32)
    row_keep = (1.0 - row_frac.astype(jnp.float32)).astype(jnp.bfloat16)
    col_keep = (1.0 - col_frac.astype(jnp.float32)).astype(jnp.bfloat16)
    base = ref_feat.astype(jnp.float32)

    def plane_variance(depth):
        taps = row_tap[:, depth].astype(jnp.int32)
        upper = jax.vmap(lambda source, index: source[:, index, :])(src_feat, taps)
        lower = jax.vmap(lambda source, index: source[:, index, :])(src_feat, taps + 1)
        keep_rows = row_keep[:, depth][:, None, :, None].astype(jnp.float32)
        frac_rows = row_frac[:, depth][:, None, :, None].astype(jnp.float32)
        rowmix = (keep_rows * upper.astype(jnp.float32) + frac_rows * lower.astype(jnp.float32)).astype(jnp.bfloat16)
        col_taps = col_tap[:, depth].astype(jnp.int32)
        left_cols = jax.vmap(lambda mixed, index: mixed[:, :, index])(rowmix, col_taps)
        right_cols = jax.vmap(lambda mixed, index: mixed[:, :, index])(rowmix, col_taps + 1)
        keep_cols = col_keep[:, depth][:, None, None, :].astype(jnp.float32)
        frac_cols = col_frac[:, depth][:, None, None, :].astype(jnp.float32)
        warped = keep_cols * left_cols.astype(jnp.float32) + frac_cols * right_cols.astype(jnp.float32)
        masked = warped * valid[:, None, :, None]
        total = base + jnp.sum(masked, axis=0)
        squares = base * base + jnp.sum(masked * warped, axis=0)
        mean_value = total / divisor[None, :, None]
        return (squares / divisor[None, :, None] - mean_value * mean_value).astype(jnp.bfloat16)

    variances = lax.map(plane_variance, jnp.arange(PLANES, dtype=jnp.int32))
    padded_stack = jnp.pad(variances, ((1, 1), (0, 0), (1, 1), (0, 0)))

    def finish(depth):
        trio = tuple(stacked_columns(lax.dynamic_index_in_dim(padded_stack, depth + shift_by, 0, keepdims=False)) for shift_by in range(3))
        result = row_term(trio, weight_mats, 0)[:, 0:HEIGHT]
        result = result + row_term(trio, weight_mats, 1)[:, 1:HEIGHT + 1]
        result = result + row_term(trio, weight_mats, 2)[:, 2:HEIGHT + 2]
        return (result + conv_bias[:, None, None]).astype(jnp.bfloat16)

    return lax.map(finish, jnp.arange(PLANES, dtype=jnp.int32))
```

```python
import jax
import jax.numpy as jnp
from jax import lax
from jax.experimental import pallas as pl
from jax.experimental.pallas import tpu as pltpu
from jax.sharding import PartitionSpec as P

VMEM_LIMIT = 56 * 1024 * 1024
CHUNKS = (16, 16)
LANES = 128


def routed(x, target):
    length = lax.axis_size("tile")
    pairs = [(i, target(i)) for i in range(length) if 0 <= target(i) < length]
    return lax.ppermute(x, "tile", pairs)


def onward(i):
    return i + 4 if i % 4 < 2 else i - 4


def gathered(block):
    across = routed(block, lambda i: i ^ 2)
    beside = routed(block, lambda i: i ^ 1)
    along = routed(across, onward)
    return [
        block,
        beside,
        across,
        routed(across, lambda i: i ^ 1),
        along,
        routed(along, lambda i: i ^ 1),
    ]


def strip_offsets(tile):
    low = (tile % 4) < 2
    across = jnp.where(low, 2, -2)
    along = -across
    beside = jnp.where(tile % 2 == 0, 1, -1)
    return jnp.stack([tile, tile + beside, tile + across, tile + beside + across, tile + along, tile + beside + along])


def warp_kernel(strips, views, planes, chans, rows, cols, *refs):
    inv_ref, refs = refs[0], refs[1:]
    strip_refs, refs = refs[:strips], refs[strips:]
    base_ref, rowmat_ref, tap_ref, frac_ref, var_ref, edge_ref, rowmix = refs
    count = chans * rows
    half = rows // 2

    def mix_rows(c, _):
        for v in range(views):
            band = jnp.concatenate([s[v, c] for s in strip_refs], axis=0)
            mixed = jnp.dot(rowmat_ref[v], band, preferred_element_type=jnp.float32)
            rowmix[v, :, pl.ds(pl.multiple_of(c * rows, rows), rows), :] = mixed.astype(jnp.bfloat16).reshape(
                planes, rows, cols
            )
        return 0

    lax.fori_loop(0, chans, mix_rows, 0)
    inv = inv_ref[0, 0]
    index = lax.broadcasted_iota(jnp.int32, (cols, cols), 0).astype(jnp.bfloat16)

    def plane(d, _):
        base = base_ref[...].reshape(count, cols).astype(jnp.float32)
        total = base
        squares = base * base
        for v in range(views):
            tap = tap_ref[v, pl.ds(d, 1), :].astype(jnp.float32)
            frac = frac_ref[v, pl.ds(d, 1), :]
            mat = jnp.where(
                index == tap.astype(jnp.bfloat16),
                (1.0 - frac).astype(jnp.bfloat16),
                jnp.where(
                    index == (tap + 1.0).astype(jnp.bfloat16), frac.astype(jnp.bfloat16), jnp.zeros((), jnp.bfloat16)
                ),
            )
            warped = jnp.dot(rowmix[v, d], mat, preferred_element_type=jnp.float32)
            total = total + warped
            squares = squares + warped * warped
        mean = total * inv
        var = (squares * inv - mean * mean).reshape(chans, 2, half, cols)
        for h in range(2):
            var_ref[d, h] = var[:, h].reshape(chans * half, cols).astype(jnp.bfloat16)
            edge_ref[h, d] = var[:, h, h * (half - 1)].astype(jnp.bfloat16)
        return 0

    lax.fori_loop(0, planes, plane, 0)


def warp(inv, strips, base, rowmat, tap, frac):
    views, chans, rows, cols = strips[0].shape
    planes = tap.shape[1]
    vmem = pl.BlockSpec(memory_space=pltpu.VMEM)

    def kernel(*refs):
        warp_kernel(len(strips), views, planes, chans, rows, cols, *refs)

    return pl.pallas_call(
        kernel,
        out_shape=(
            jax.ShapeDtypeStruct((planes, 2, chans * rows // 2, cols), jnp.bfloat16),
            jax.ShapeDtypeStruct((2, planes, chans, cols), jnp.bfloat16),
        ),
        in_specs=[pl.BlockSpec(memory_space=pltpu.SMEM)] + [vmem] * (len(strips) + 4),
        out_specs=(vmem, vmem),
        scratch_shapes=[pltpu.VMEM((views, planes, chans * rows, cols), jnp.bfloat16)],
        compiler_params=pltpu.CompilerParams(vmem_limit_bytes=VMEM_LIMIT),
        cost_estimate=pl.CostEstimate(
            flops=2 * views * planes * chans * rows * cols * cols * 2, bytes_accessed=4 << 20, transcendentals=0
        ),
        name="warp",
    )(inv, *strips, base, rowmat, tap, frac)


def joined_columns(parts):
    left, middle, right = parts
    cols = middle.shape[-1]
    lane = lax.broadcasted_iota(jnp.int32, middle.shape, middle.ndim - 1)
    left = jnp.where(lane == 0, 0.0, pltpu.roll(left, 1, middle.ndim - 1))
    right = jnp.where(lane == cols - 1, 0.0, pltpu.roll(right, cols - 1, middle.ndim - 1))
    return middle + left + right


def edge_kernel(planes, group, outs, cols, nchunks, *refs):
    edge_refs, (mat_ref, up_ref, down_ref, acc) = refs[:nchunks], refs[nchunks:]
    for side, out in ((0, up_ref), (1, down_ref)):
        acc[...] = jnp.zeros_like(acc)
        for start in range(0, planes, group):
            terms = jnp.zeros((3 * (group + 2) * outs, cols), jnp.float32)
            offset = 0
            for edge in edge_refs:
                chans = edge.shape[2]
                rhs = edge[side, start : start + group].reshape(group * chans, cols)
                lhs = mat_ref[side, :, offset * group : (offset + chans) * group]
                terms = terms + jnp.dot(lhs, rhs, preferred_element_type=jnp.float32)
                offset += chans
            rows = (group + 2) * outs
            acc[start * outs : start * outs + rows] += joined_columns([terms[e * rows : (e + 1) * rows] for e in range(3)])
        out[...] = acc[outs : outs + planes * outs].astype(jnp.bfloat16)


def edge_terms(edges, mat, outs):
    planes, cols = edges[0].shape[1], edges[0].shape[3]
    group = mat.shape[1] // (3 * outs) - 2
    vmem = pl.BlockSpec(memory_space=pltpu.VMEM)

    def kernel(*refs):
        edge_kernel(planes, group, outs, cols, len(edges), *refs)

    shape = jax.ShapeDtypeStruct((planes * outs, cols), jnp.bfloat16)
    return pl.pallas_call(
        kernel,
        out_shape=(shape, shape),
        in_specs=[vmem] * (len(edges) + 1),
        out_specs=(vmem, vmem),
        scratch_shapes=[pltpu.VMEM(((planes + 2) * outs, cols), jnp.float32)],
        compiler_params=pltpu.CompilerParams(vmem_limit_bytes=VMEM_LIMIT),
        name="edge",
    )(*edges, mat)


def filter_kernel(planes, rows, outs, cols, nchunks, *refs):
    bias_ref, refs = refs[0], refs[1:]
    var_refs, (mat_ref, above_ref, below_ref, out_ref, flat) = refs[:nchunks], refs[nchunks:]
    half = rows // 2
    depth = mat_ref.shape[2] // 3
    width = (half + 1) * outs

    def plane(d, taps):
        parts = []
        for h in range(2):
            rhs = jnp.concatenate([v[d + a - 1, h] for a in taps for v in var_refs], axis=0)
            lhs = mat_ref[h, :, taps[0] * depth : (taps[-1] + 1) * depth]
            terms = jnp.dot(lhs, rhs, preferred_element_type=jnp.float32)
            parts.append(joined_columns([terms[e * width : (e + 1) * width] for e in range(3)]))
        upper, lower = parts
        at = pl.multiple_of(d * outs, outs)
        upper = upper + jnp.concatenate([above_ref[pl.ds(at, outs), :].astype(jnp.float32), jnp.zeros((half * outs, cols))])
        lower = lower + jnp.concatenate([jnp.zeros((half * outs, cols)), below_ref[pl.ds(at, outs), :].astype(jnp.float32)])
        whole = jnp.concatenate(
            [
                upper[: (half - 1) * outs],
                upper[(half - 1) * outs :] + lower[: 2 * outs],
                lower[2 * outs :],
            ]
        )
        for lane in range(cols // LANES):
            lanes = slice(lane * LANES, (lane + 1) * LANES)
            flat[lane] = whole[:, lanes]
            for o in range(outs):
                out_ref[d, o, :, lanes] = (flat[lane, pl.ds(o, rows, stride=outs), :] + bias_ref[0, o]).astype(jnp.bfloat16)

    plane(0, (1, 2))

    def inner(d, _):
        plane(d, (0, 1, 2))
        return 0

    lax.fori_loop(1, planes - 1, inner, 0)
    plane(planes - 1, (0, 1))


def filtered(bias, variances, mat, above, below, rows, outs):
    planes, _, _, cols = variances[0].shape
    vmem = pl.BlockSpec(memory_space=pltpu.VMEM)

    def kernel(*refs):
        filter_kernel(planes, rows, outs, cols, len(variances), *refs)

    return pl.pallas_call(
        kernel,
        out_shape=jax.ShapeDtypeStruct((planes, outs, rows, cols), jnp.bfloat16),
        in_specs=[pl.BlockSpec(memory_space=pltpu.SMEM)] + [vmem] * (len(variances) + 3),
        out_specs=vmem,
        scratch_shapes=[pltpu.VMEM((cols // LANES, rows * outs, LANES), jnp.float32)],
        compiler_params=pltpu.CompilerParams(vmem_limit_bytes=VMEM_LIMIT),
        name="filter",
    )(bias, *variances, mat, above, below)


def filter_matrix(weight, half):
    outs, chans = weight.shape[3:]
    mats = []
    for h in range(2):
        target = jnp.arange(half + 1) - h
        tap = jnp.arange(half)[None, :] - target[:, None] + 1
        pick = (tap[:, :, None] == jnp.arange(3)).astype(weight.dtype)
        mats.append(jnp.einsum("grb,abeoc->egoacr", pick, weight).reshape(3 * (half + 1) * outs, 3 * chans * half))
    return jnp.stack(mats)


def edge_matrix(weight, chunks, group):
    outs, chans = weight.shape[3:]
    tap = jnp.arange(group)[None, :] - jnp.arange(group + 2)[:, None] + 2
    pick = (tap[:, :, None] == jnp.arange(3)).astype(weight.dtype)
    sides = []
    for b in (2, 0):
        parts = []
        offset = 0
        for size in chunks:
            part = weight[:, b, :, :, offset : offset + size]
            parts.append(jnp.einsum("pqa,aeoc->epoqc", pick, part).reshape(3 * (group + 2) * outs, group * size))
            offset += size
        sides.append(jnp.concatenate(parts, axis=1))
    return jnp.stack(sides)


def on_device(
    ref_feat, src_feat, row_tap, row_frac, col_tap, col_frac, view_count, conv_weight, conv_bias
):
    rows = ref_feat.shape[1]
    views = src_feat.shape[0]
    planes = row_tap.shape[1]
    outs = conv_weight.shape[3]
    tile = lax.axis_index("tile")

    starts = strip_offsets(tile) * rows
    index = (starts[:, None] + jnp.arange(rows)).reshape(-1)
    keep = (1.0 - row_frac.astype(jnp.float32)).astype(jnp.bfloat16)
    valid = (jnp.arange(views) < view_count[0])[:, None, None, None]
    zero = jnp.zeros((), jnp.bfloat16)
    rowmat = jnp.where(
        (index == row_tap[..., None]) & valid,
        keep[..., None],
        jnp.where((index == row_tap[..., None] + 1) & valid, row_frac[..., None], zero),
    ).reshape(views, planes * rows, -1)
    inv = (1.0 / (1.0 + view_count.astype(jnp.float32))).reshape(1, 1)
    frac = col_frac.astype(jnp.float32)
    filter_mat = filter_matrix(conv_weight, rows // 2)
    edge_mat = edge_matrix(conv_weight, CHUNKS, 8)

    variances = []
    edges = []
    offset = 0
    for size in CHUNKS:
        strips = gathered(src_feat[:, offset : offset + size])
        var, edge = warp(inv, strips, ref_feat[offset : offset + size], rowmat, col_tap, frac)
        variances.append(var)
        edges.append(edge)
        offset += size
    up, down = edge_terms(edges, edge_mat, outs)
    above = routed(down, lambda i: i + 1)
    below = routed(up, lambda i: i - 1)
    return filtered(conv_bias.reshape(1, -1), variances, filter_mat, above, below, rows, outs)


def solution(mesh):
    placed = (
        P("groups", "tile", None),
        P("groups", None, "tile", None),
        P("groups", None, "tile"),
        P("groups", None, "tile"),
        P("groups", None, None),
        P("groups", None, None),
        P(("groups", "tile")),
        P(),
        P(),
    )
    return jax.shard_map(
        on_device,
        mesh=mesh,
        in_specs=placed,
        out_specs=P("groups", None, "tile", None),
        check_vma=False,
    )
```

```python
import jax
import jax.numpy as jnp
from jax import lax
from jax.experimental import pallas as pl
from jax.experimental.pallas import tpu as pltpu
from jax.sharding import PartitionSpec as P

MIB = 1024 * 1024
CHUNKS = (16, 16)
LANES = 128
WIDE = 8
UNROLL = 4
GROUP = 8


def routed(x, target):
    length = lax.axis_size("tile")
    pairs = [(i, target(i)) for i in range(length) if 0 <= target(i) < length]
    return lax.ppermute(x, "tile", pairs)


def onward(i):
    return i + 4 if i % 4 < 2 else i - 4


def strip_offsets(tile):
    low = (tile % 4) < 2
    across = jnp.where(low, 2, -2)
    along = -across
    beside = jnp.where(tile % 2 == 0, 1, -1)
    return jnp.stack([tile, tile + beside, tile + across, tile + beside + across, tile + along, tile + beside + along])


def column_kernel(views, cols, tap_ref, frac_ref, out_ref):
    index = lax.broadcasted_iota(jnp.int32, (cols, cols), 0).astype(jnp.bfloat16)
    zero = jnp.zeros((), jnp.bfloat16)

    def plane(d, _):
        for v in range(views):
            tap = tap_ref[v, pl.ds(d, 1), :]
            frac = frac_ref[v, pl.ds(d, 1), :]
            upper = jnp.where(index == (tap + 1.0).astype(jnp.bfloat16), frac.astype(jnp.bfloat16), zero)
            out_ref[d, v] = jnp.where(index == tap.astype(jnp.bfloat16), (1.0 - frac).astype(jnp.bfloat16), upper)
        return 0

    lax.fori_loop(0, tap_ref.shape[1], plane, 0)


def column_matrices(tap, frac):
    views, planes, cols = tap.shape
    vmem = pl.BlockSpec(memory_space=pltpu.VMEM)

    def kernel(*refs):
        column_kernel(views, cols, *refs)

    return pl.pallas_call(
        kernel,
        out_shape=jax.ShapeDtypeStruct((planes, views, cols, cols), jnp.bfloat16),
        in_specs=[vmem, vmem],
        out_specs=vmem,
        compiler_params=pltpu.CompilerParams(vmem_limit_bytes=20 * MIB),
        name="columns",
    )(tap, frac)


def warp_kernel(strips, views, planes, chans, rows, cols, *refs):
    inv_ref, refs = refs[0], refs[1:]
    strip_refs, refs = refs[:strips], refs[strips:]
    base_ref, rowmat_ref, colmat_ref, var_ref, edge_ref, rowmix, even, odd = refs
    count = chans * rows
    half = rows // 2
    depth = rowmat_ref.shape[2]
    wide = max(w for w in range(1, WIDE + 1) if chans % w == 0)
    blank = jnp.zeros((depth - strips * rows, cols), jnp.bfloat16)

    def mix_rows(c, _):
        for v in range(views):
            bands = [
                jnp.concatenate([s[v, c * wide + k] for s in strip_refs] + [blank], axis=0) for k in range(wide)
            ]
            band = jnp.concatenate(bands, axis=1)
            for start in range(0, planes, 8):
                lhs = rowmat_ref[v, start * rows : (start + 8) * rows, :]
                mixed = jnp.dot(lhs, band, preferred_element_type=jnp.float32).astype(jnp.bfloat16)
                for k in range(wide):
                    at = pl.ds(pl.multiple_of((c * wide + k) * rows, rows), rows)
                    rowmix[v, start : start + 8, at, :] = mixed[:, k * cols : (k + 1) * cols].reshape(8, rows, cols)
        return 0

    lax.fori_loop(0, chans // wide, mix_rows, 0)
    inv = inv_ref[0, 0]

    def warp_plane(d, warped):
        for v in range(views):
            warped[v] = jnp.dot(rowmix[v, d], colmat_ref[d, v], preferred_element_type=jnp.float32)

    def finish_plane(d, warped):
        for c in range(0, chans, 2):
            total = base_ref[c : c + 2].reshape(2 * rows, cols)
            squares = total * total
            for v in range(views):
                term = warped[v, c * rows : (c + 2) * rows, :]
                total = total + term
                squares = squares + term * term
            var = (squares - total * (total * inv)).reshape(2, 2, half, cols)
            for h in range(2):
                var_ref[d, h, c * half : (c + 2) * half, :] = var[:, h].reshape(2 * half, cols).astype(jnp.bfloat16)
                edge_ref[h, d, c : c + 2, :] = var[:, h, h * (half - 1)]

    slots = (even, odd)
    warp_plane(0, even)

    def step(i, _):
        for k in range(UNROLL):
            d = i * UNROLL + k
            warp_plane(jnp.minimum(d + 1, planes - 1), slots[(k + 1) % 2])
            finish_plane(d, slots[k % 2])
        return 0

    lax.fori_loop(0, planes // UNROLL, step, 0)


def warp(inv, strips, base, rowmat, colmat):
    views, size, rows, cols = strips[0].shape
    planes = colmat.shape[0]
    vmem = pl.BlockSpec(memory_space=pltpu.VMEM)

    def kernel(*refs):
        warp_kernel(len(strips), views, planes, size, rows, cols, *refs)

    return pl.pallas_call(
        kernel,
        out_shape=(
            jax.ShapeDtypeStruct((planes, 2, size * rows // 2, cols), jnp.bfloat16),
            jax.ShapeDtypeStruct((2, planes, size, cols), jnp.float32),
        ),
        in_specs=[pl.BlockSpec(memory_space=pltpu.SMEM)] + [vmem] * (len(strips) + 3),
        out_specs=(vmem, vmem),
        scratch_shapes=[
            pltpu.VMEM((views, planes, size * rows, cols), jnp.bfloat16),
            pltpu.VMEM((views, size * rows, cols), jnp.float32),
            pltpu.VMEM((views, size * rows, cols), jnp.float32),
        ],
        compiler_params=pltpu.CompilerParams(vmem_limit_bytes=22 * MIB),
        cost_estimate=pl.CostEstimate(
            flops=2 * views * planes * size * rows * cols * cols * 2, bytes_accessed=4 << 20, transcendentals=0
        ),
        name="warp",
    )(inv, *strips, base, rowmat, colmat)


def joined_columns(terms, outs):
    cols = terms.shape[-1]
    terms = terms.reshape(-1, 3, outs, cols)
    left, middle, right = [terms[:, e].reshape(-1, cols) for e in range(3)]
    lane = lax.broadcasted_iota(jnp.int32, middle.shape, 1)
    left = jnp.where(lane == 0, 0.0, pltpu.roll(left, 1, 1))
    right = jnp.where(lane == cols - 1, 0.0, pltpu.roll(right, cols - 1, 1))
    return middle + left + right


def edge_kernel(planes, group, outs, cols, nchunks, inv_ref, *refs):
    edge_refs, (mat_ref, up_ref, down_ref, acc) = refs[:nchunks], refs[nchunks:]
    for side, out in ((0, up_ref), (1, down_ref)):
        acc[...] = jnp.zeros_like(acc)
        for start in range(0, planes, group):
            rhs = jnp.concatenate([e[side, start : start + group].reshape(-1, cols) for e in edge_refs], axis=0)
            terms = jnp.dot(mat_ref[side], rhs.astype(jnp.bfloat16), preferred_element_type=jnp.float32)
            rows = (group + 2) * outs
            acc[start * outs : start * outs + rows] += joined_columns(terms, outs)
        out[...] = (acc[outs : outs + planes * outs] * inv_ref[0, 0]).astype(jnp.bfloat16)


def edge_terms(inv, edges, mat, outs):
    planes, cols = edges[0].shape[1], edges[0].shape[3]
    group = mat.shape[1] // (3 * outs) - 2
    vmem = pl.BlockSpec(memory_space=pltpu.VMEM)

    def kernel(*refs):
        edge_kernel(planes, group, outs, cols, len(edges), *refs)

    shape = jax.ShapeDtypeStruct((planes * outs, cols), jnp.bfloat16)
    return pl.pallas_call(
        kernel,
        out_shape=(shape, shape),
        in_specs=[pl.BlockSpec(memory_space=pltpu.SMEM)] + [vmem] * (len(edges) + 1),
        out_specs=(vmem, vmem),
        scratch_shapes=[pltpu.VMEM(((planes + 2) * outs, cols), jnp.float32)],
        compiler_params=pltpu.CompilerParams(vmem_limit_bytes=16 * MIB),
        name="edge",
    )(inv, *edges, mat)


def filter_kernel(planes, start, count, rows, outs, cols, nchunks, *refs):
    inv_ref, bias_ref, refs = refs[0], refs[1], refs[2:]
    var_refs, refs = refs[:nchunks], refs[nchunks:]
    first = start == 0
    if first:
        mat_ref, out_ref = refs
    else:
        mat_ref, early_ref, above_ref, below_ref, out_ref, *flats = refs
    half = rows // 2
    inv = inv_ref[0, 0]

    def block(d, h, exists):
        found = jnp.concatenate([v[d, h] for v in var_refs], axis=0)
        return found if exists is None else found * exists.astype(jnp.float32).astype(jnp.bfloat16)

    def sums(d, k):
        parts = []
        for h in range(2):
            before = block(jnp.maximum(d - 1, 0), h, d > 0 if first and k == 0 else None)
            after = block(jnp.minimum(d + 1, planes - 1), h, d < planes - 1 if not first and k == UNROLL - 1 else None)
            rhs = jnp.concatenate([before, block(d, h, None), after], axis=0)
            terms = jnp.dot(mat_ref[h], rhs, preferred_element_type=jnp.float32)
            parts.append(joined_columns(terms, outs) * inv)
        upper, lower = parts
        return jnp.concatenate(
            [upper[: (half - 1) * outs], upper[(half - 1) * outs :] + lower[: 2 * outs], lower[2 * outs :]]
        )

    def finish(d, whole, flat):
        at = pl.multiple_of(d * outs, outs)
        whole = jnp.concatenate(
            [
                whole[:outs] + above_ref[pl.ds(at, outs), :].astype(jnp.float32),
                whole[outs:-outs],
                whole[-outs:] + below_ref[pl.ds(at, outs), :].astype(jnp.float32),
            ]
        )
        for lane in range(cols // LANES):
            lanes = slice(lane * LANES, (lane + 1) * LANES)
            flat[lane] = whole[:, lanes]
            for o in range(outs):
                out_ref[d, o, :, lanes] = (flat[lane, pl.ds(o, rows, stride=outs), :] + bias_ref[0, o]).astype(jnp.bfloat16)

    def step(i, _):
        for k in range(UNROLL):
            at = i * UNROLL + k
            whole = sums(start + at, k)
            if first:
                out_ref[at] = whole
            else:
                finish(at, early_ref[at], flats[2 * k])
                finish(start + at, whole, flats[2 * k + 1])
        return 0

    lax.fori_loop(0, count // UNROLL, step, 0)


def filtered(inv, bias, variances, mat, rows, outs, early=None, above=None, below=None):
    planes, _, _, cols = variances[0].shape
    vmem = pl.BlockSpec(memory_space=pltpu.VMEM)
    smem = pl.BlockSpec(memory_space=pltpu.SMEM)
    count = planes // 2
    first = early is None
    more = [] if first else [early, above, below]

    def kernel(*refs):
        filter_kernel(planes, 0 if first else count, count, rows, outs, cols, len(variances), *refs)

    return pl.pallas_call(
        kernel,
        out_shape=jax.ShapeDtypeStruct((count, rows * outs, cols), jnp.float32)
        if first
        else jax.ShapeDtypeStruct((planes, outs, rows, cols), jnp.bfloat16),
        in_specs=[smem, smem] + [vmem] * (len(variances) + 1 + len(more)),
        out_specs=vmem,
        scratch_shapes=[]
        if first
        else [pltpu.VMEM((cols // LANES, rows * outs, LANES), jnp.float32)] * (2 * UNROLL),
        compiler_params=pltpu.CompilerParams(vmem_limit_bytes=20 * MIB),
        cost_estimate=pl.CostEstimate(
            flops=2 * count * 2 * mat.shape[1] * mat.shape[2] * cols, bytes_accessed=8 << 20, transcendentals=0
        ),
        name="filter",
    )(inv, bias, *variances, mat, *more)


def matrix_kernel(chunks, group, weight_ref, filter_ref, edge_ref):
    taps, each, chans = weight_ref.shape
    half = filter_ref.shape[1] // each - 1
    width = chans * half
    weight = weight_ref[...].reshape(taps * each, chans)
    chan = lax.broadcasted_iota(jnp.int32, (chans, width), 0)
    lane = lax.broadcasted_iota(jnp.int32, (chans, width), 1)

    def spread(mask):
        onehot = jnp.where(mask, 1.0, 0.0).astype(jnp.bfloat16)
        return jnp.dot(weight, onehot, preferred_element_type=jnp.float32).reshape(taps, each, width)

    by_row = [spread(lane == chan * half + r) for r in range(half)]
    for h in range(2):
        for a in range(3):
            rows = []
            for g in range(half + 1):
                row = jnp.zeros((each, width), jnp.float32)
                for b in range(3):
                    r = g - h + b - 1
                    if 0 <= r < half:
                        row = row + by_row[r][3 * a + b]
                rows.append(row)
            filter_ref[h, :, a * width : (a + 1) * width] = jnp.concatenate(rows).astype(jnp.bfloat16)
    by_plane = []
    for q in range(group):
        mask = chan < 0
        offset = 0
        for size in chunks:
            here = (chan >= offset) & (chan < offset + size)
            mask = mask | (here & (lane == chan + offset * (group - 1) + q * size))
            offset += size
        by_plane.append(spread(mask))
    for side, b in ((0, 2), (1, 0)):
        rows = []
        for p in range(group + 2):
            row = jnp.zeros((each, width), jnp.float32)
            for a in range(3):
                q = a + p - 2
                if 0 <= q < group:
                    row = row + by_plane[q][3 * a + b]
            rows.append(row)
        edge_ref[side] = jnp.concatenate(rows).astype(jnp.bfloat16)


def matrices(weight, rows, chunks, group):
    outs, chans = weight.shape[3:]
    each = 3 * outs
    half = rows // 2
    vmem = pl.BlockSpec(memory_space=pltpu.VMEM)

    def kernel(*refs):
        matrix_kernel(chunks, group, *refs)

    return pl.pallas_call(
        kernel,
        out_shape=(
            jax.ShapeDtypeStruct((2, (half + 1) * each, 3 * chans * half), jnp.bfloat16),
            jax.ShapeDtypeStruct((2, (group + 2) * each, group * chans), jnp.bfloat16),
        ),
        in_specs=[vmem],
        out_specs=(vmem, vmem),
        compiler_params=pltpu.CompilerParams(vmem_limit_bytes=16 * MIB),
        name="matrices",
    )(weight.reshape(9, each, chans))


def on_device(
    ref_feat, src_feat, row_tap, row_frac, col_tap, col_frac, view_count, conv_weight, conv_bias
):
    rows = ref_feat.shape[1]
    views = src_feat.shape[0]
    planes = row_tap.shape[1]
    outs = conv_weight.shape[3]
    tile = lax.axis_index("tile")

    starts = strip_offsets(tile) * rows
    index = (starts[:, None] + jnp.arange(rows)).reshape(-1)
    index = jnp.pad(index, (0, LANES - index.shape[0]), constant_values=-2)
    keep = (1.0 - row_frac.astype(jnp.float32)).astype(jnp.bfloat16)
    valid = (jnp.arange(views) < view_count[0])[:, None, None, None]
    zero = jnp.zeros((), jnp.bfloat16)
    rowmat = jnp.where(
        (index == row_tap[..., None]) & valid,
        keep[..., None],
        jnp.where((index == row_tap[..., None] + 1) & valid, row_frac[..., None], zero),
    ).reshape(views, planes * rows, -1)
    inv = (1.0 / (1.0 + view_count.astype(jnp.float32))).reshape(1, 1)
    frac = col_frac.astype(jnp.float32)
    colmat = column_matrices(col_tap.astype(jnp.float32), frac)
    base = ref_feat.astype(jnp.float32)
    filter_mat, edge_mat = matrices(conv_weight, rows, CHUNKS, GROUP)

    spans = [slice(sum(CHUNKS[:i]), sum(CHUNKS[: i + 1])) for i in range(len(CHUNKS))]
    pieces = [src_feat[:, span] for span in spans]
    pieces[1:] = lax.optimization_barrier(pieces[1:])
    across = [routed(piece, lambda i: i ^ 2) for piece in pieces]
    beside = [routed(piece, lambda i: i ^ 1) for piece in pieces]
    bases = [base[span] for span in spans]
    across[0], rowmat, colmat, bases, filter_mat, edge_mat = lax.optimization_barrier(
        (across[0], rowmat, colmat, bases, filter_mat, edge_mat)
    )
    variances = []
    edges = []
    along = routed(across[0], onward)
    across_beside = routed(across[0], lambda i: i ^ 1)
    for i in range(len(CHUNKS)):
        along_beside = routed(along, lambda i: i ^ 1)
        strips = [pieces[i], beside[i], across[i], across_beside, along, along_beside]
        if i + 1 < len(CHUNKS):
            along = routed(across[i + 1], onward)
            across_beside = routed(across[i + 1], lambda i: i ^ 1)
        var, edge = warp(inv, strips, bases[i], rowmat, colmat)
        if i + 1 < len(CHUNKS):
            var, edge, along, across_beside, across[i + 2 :] = lax.optimization_barrier(
                (var, edge, along, across_beside, across[i + 2 :])
            )
        variances.append(var)
        edges.append(edge)
    up, down = edge_terms(inv, edges, edge_mat, outs)
    above = routed(down, lambda i: i + 1)
    below = routed(up, lambda i: i - 1)
    bias = conv_bias.reshape(1, -1)
    early = filtered(inv, bias, variances, filter_mat, rows, outs)
    return filtered(inv, bias, variances, filter_mat, rows, outs, early, above, below)


def solution(mesh):
    placed = (
        P("groups", "tile", None),
        P("groups", None, "tile", None),
        P("groups", None, "tile"),
        P("groups", None, "tile"),
        P("groups", None, None),
        P("groups", None, None),
        P(("groups", "tile")),
        P(),
        P(),
    )
    return jax.shard_map(
        on_device,
        mesh=mesh,
        in_specs=placed,
        out_specs=P("groups", None, "tile", None),
        check_vma=False,
    )
```

```python
import jax
import jax.numpy as jnp
from jax import lax
from jax.experimental import pallas as pl
from jax.experimental.pallas import tpu as pltpu
from jax.sharding import PartitionSpec as P

MIB = 1024 * 1024
PARTS = ((8,), (12,), (12,))
CHUNKS = tuple(sum(sizes) for sizes in PARTS)
LANES = 128
WIDE = 16
UNROLL = 4
GROUP = 8


def routed(x, target):
    length = lax.axis_size("tile")
    pairs = [(i, target(i)) for i in range(length) if 0 <= target(i) < length]
    return lax.ppermute(x, "tile", pairs)


def onward(i):
    return i + 4 if i % 4 < 2 else i - 4


def strip_offsets(tile):
    across = jnp.where(lax.rem(tile, 4) < 2, 2, -2)
    beside = jnp.where(lax.rem(tile, 2) == 0, 1, -1)
    return [tile, tile + beside, tile + across, tile + beside + across, tile - across, tile + beside - across]


def table_kernel(rows, tile_ref, count_ref, row_tap_ref, row_frac_ref, tap_ref, frac_ref, rowmat_ref, colmat_ref, taps, fracs):
    views, planes, cols = tap_ref.shape
    zero = jnp.zeros((), jnp.bfloat16)
    tile = tile_ref[0, 0]
    lane = lax.broadcasted_iota(jnp.int32, (rows, LANES), 1)
    band = jnp.full((rows, LANES), -2, jnp.int32)
    for slot, strip in enumerate(strip_offsets(tile)):
        here = (lane >= slot * rows) & (lane < (slot + 1) * rows)
        band = jnp.where(here, lane + (strip - slot) * rows, band)
    for v in range(views):
        scale = jnp.where(v < count_ref[0, 0], 1.0, 0.0)
        for d in range(planes):
            tap = row_tap_ref[v, :, d : d + 1]
            frac = row_frac_ref[v, :, d : d + 1].astype(jnp.float32)
            keep = 1.0 - frac
            mat = jnp.where(band == tap, keep * scale, jnp.where(band == tap + 1, frac * scale, 0.0))
            rowmat_ref[v, d * rows : (d + 1) * rows, :] = mat.astype(jnp.bfloat16)
    taps[...] = tap_ref[...].astype(jnp.float32)
    fracs[...] = frac_ref[...].astype(jnp.float32)
    index = lax.broadcasted_iota(jnp.int32, (cols, cols), 0).astype(jnp.bfloat16)

    def plane(d, _):
        for v in range(views):
            tap = taps[v, pl.ds(d, 1), :]
            frac = fracs[v, pl.ds(d, 1), :]
            upper = jnp.where(index == (tap + 1.0).astype(jnp.bfloat16), frac.astype(jnp.bfloat16), zero)
            colmat_ref[d, v] = jnp.where(index == tap.astype(jnp.bfloat16), (1.0 - frac).astype(jnp.bfloat16), upper)
        return 0

    lax.fori_loop(0, planes, plane, 0)


def tables(tile, view_count, row_tap, row_frac, col_tap, col_frac):
    views, planes, cols = col_tap.shape
    rows = row_tap.shape[2]
    vmem = pl.BlockSpec(memory_space=pltpu.VMEM)
    smem = pl.BlockSpec(memory_space=pltpu.SMEM)

    def kernel(*refs):
        table_kernel(rows, *refs)

    return pl.pallas_call(
        kernel,
        out_shape=(
            jax.ShapeDtypeStruct((views, planes * rows, LANES), jnp.bfloat16),
            jax.ShapeDtypeStruct((planes, views, cols, cols), jnp.bfloat16),
        ),
        in_specs=[smem, smem] + [vmem] * 4,
        out_specs=(vmem, vmem),
        scratch_shapes=[pltpu.VMEM((views, planes, cols), jnp.float32)] * 2,
        compiler_params=pltpu.CompilerParams(vmem_limit_bytes=20 * MIB),
        name="tables",
    )(
        tile.reshape(1, 1).astype(jnp.int32),
        view_count.reshape(1, 1),
        jnp.swapaxes(row_tap, 1, 2),
        jnp.swapaxes(row_frac, 1, 2),
        col_tap,
        col_frac,
    )


def warp_kernel(strips, sizes, views, planes, chans, rows, cols, *refs):
    inv_ref, refs = refs[0], refs[1:]
    strip_refs, refs = refs[: strips * len(sizes)], refs[strips * len(sizes) :]
    base_ref, rowmat_ref, colmat_ref, var_ref, edge_ref, rowmix, even, odd = refs
    count = chans * rows
    half = rows // 2
    depth = rowmat_ref.shape[2]
    blank = jnp.zeros((depth - strips * rows, cols), jnp.bfloat16)

    def mix_rows(part, offset, wide, v, c):
        refs_here = strip_refs[part :: len(sizes)]
        bands = [
            jnp.concatenate([ref[v, c * wide + k] for ref in refs_here] + [blank], axis=0) for k in range(wide)
        ]
        band = jnp.concatenate(bands, axis=1)
        for start in range(0, planes, 8):
            lhs = rowmat_ref[v, start * rows : (start + 8) * rows, :]
            mixed = jnp.dot(lhs, band, preferred_element_type=jnp.float32).astype(jnp.bfloat16)
            for k in range(wide):
                at = pl.ds(pl.multiple_of((offset + c * wide + k) * rows, rows), rows)
                rowmix[v, start : start + 8, at, :] = mixed[:, k * cols : (k + 1) * cols].reshape(8, rows, cols)

    offset = 0
    for part, size in enumerate(sizes):
        wide = max(w for w in range(1, WIDE + 1) if size % w == 0)

        def step(c, _, part=part, offset=offset, wide=wide):
            for v in range(views):
                mix_rows(part, offset, wide, v, c)
            return 0

        lax.fori_loop(0, size // wide, step, 0)
        offset += size
    inv = inv_ref[0, 0]

    held = views - 2

    def warp_view(d, v):
        return jnp.dot(rowmix[v, d], colmat_ref[d, v], preferred_element_type=jnp.float32)

    def warp_plane(d, warped):
        for v in range(held):
            warped[v] = warp_view(d, v)

    def finish_plane(d, warped):
        fresh = [warp_view(d, v) for v in range(held, views)]
        for c in range(0, chans, 2):
            here = slice(c * rows, (c + 2) * rows)
            total = base_ref[c : c + 2].reshape(2 * rows, cols)
            squares = total * total
            for term in [warped[v, here, :] for v in range(held)] + [term[here] for term in fresh]:
                total = total + term
                squares = squares + term * term
            var = (squares - total * (total * inv)).reshape(2, 2, half, cols)
            for h in range(2):
                var_ref[d, h, c * half : (c + 2) * half, :] = var[:, h].reshape(2 * half, cols).astype(jnp.bfloat16)
                edge_ref[h, d, c : c + 2, :] = var[:, h, h * (half - 1)]

    slots = (even, odd)
    warp_plane(0, even)

    def step(i, _):
        for k in range(UNROLL):
            d = i * UNROLL + k
            warp_plane(jnp.minimum(d + 1, planes - 1), slots[(k + 1) % 2])
            finish_plane(d, slots[k % 2])
        return 0

    lax.fori_loop(0, planes // UNROLL, step, 0)


def warp(inv, strips, base, rowmat, colmat):
    views, _, rows, cols = strips[0][0].shape
    sizes = [part.shape[1] for part in strips[0]]
    size = sum(sizes)
    planes = colmat.shape[0]
    vmem = pl.BlockSpec(memory_space=pltpu.VMEM)

    def kernel(*refs):
        warp_kernel(len(strips), sizes, views, planes, size, rows, cols, *refs)

    return pl.pallas_call(
        kernel,
        out_shape=(
            jax.ShapeDtypeStruct((planes, 2, size * rows // 2, cols), jnp.bfloat16),
            jax.ShapeDtypeStruct((2, planes, size, cols), jnp.float32),
        ),
        in_specs=[pl.BlockSpec(memory_space=pltpu.SMEM)] + [vmem] * (len(strips) * len(sizes) + 3),
        out_specs=(vmem, vmem),
        scratch_shapes=[
            pltpu.VMEM((views, planes, size * rows, cols), jnp.bfloat16),
            pltpu.VMEM((views, size * rows, cols), jnp.float32),
            pltpu.VMEM((views, size * rows, cols), jnp.float32),
        ],
        compiler_params=pltpu.CompilerParams(vmem_limit_bytes=22 * MIB),
        cost_estimate=pl.CostEstimate(
            flops=1 << 20, bytes_accessed=1 << 10, transcendentals=0
        ),
        name="warp",
    )(inv, *[part for strip in strips for part in strip], base, rowmat, colmat)


def joined_columns(terms, outs):
    cols = terms.shape[-1]
    terms = terms.reshape(-1, 3, outs, cols)
    left, middle, right = [terms[:, e].reshape(-1, cols) for e in range(3)]
    lane = lax.broadcasted_iota(jnp.int32, middle.shape, 1)
    left = jnp.where(lane == 0, 0.0, pltpu.roll(left, 1, 1))
    right = jnp.where(lane == cols - 1, 0.0, pltpu.roll(right, cols - 1, 1))
    return middle + left + right


def edge_kernel(planes, group, outs, cols, nchunks, inv_ref, *refs):
    edge_refs, (mat_ref, up_ref, down_ref, acc) = refs[:nchunks], refs[nchunks:]
    for side, out in ((0, up_ref), (1, down_ref)):
        acc[...] = jnp.zeros_like(acc)
        for start in range(0, planes, group):
            rhs = jnp.concatenate([e[side, start : start + group].reshape(-1, cols) for e in edge_refs], axis=0)
            terms = jnp.dot(mat_ref[side], rhs.astype(jnp.bfloat16), preferred_element_type=jnp.float32)
            rows = (group + 2) * outs
            acc[start * outs : start * outs + rows] += joined_columns(terms, outs)
        out[...] = (acc[outs : outs + planes * outs] * inv_ref[0, 0]).astype(jnp.bfloat16)


def edge_terms(inv, edges, mat, outs):
    planes, cols = edges[0].shape[1], edges[0].shape[3]
    group = mat.shape[1] // (3 * outs) - 2
    vmem = pl.BlockSpec(memory_space=pltpu.VMEM)

    def kernel(*refs):
        edge_kernel(planes, group, outs, cols, len(edges), *refs)

    shape = jax.ShapeDtypeStruct((planes * outs, cols), jnp.bfloat16)
    return pl.pallas_call(
        kernel,
        out_shape=(shape, shape),
        in_specs=[pl.BlockSpec(memory_space=pltpu.SMEM)] + [vmem] * (len(edges) + 1),
        out_specs=(vmem, vmem),
        scratch_shapes=[pltpu.VMEM(((planes + 2) * outs, cols), jnp.float32)],
        compiler_params=pltpu.CompilerParams(vmem_limit_bytes=16 * MIB),
        name="edge",
    )(inv, *edges, mat)


def filter_kernel(planes, start, count, rows, outs, cols, nchunks, *refs):
    inv_ref, bias_ref, refs = refs[0], refs[1], refs[2:]
    var_refs, refs = refs[:nchunks], refs[nchunks:]
    first = start == 0
    if first:
        mat_ref, out_ref = refs
    else:
        mat_ref, early_ref, above_ref, below_ref, out_ref, *flats = refs
    half = rows // 2
    inv = inv_ref[0, 0]

    def block(d, h, exists):
        found = jnp.concatenate([v[d, h] for v in var_refs], axis=0)
        return found if exists is None else found * exists.astype(jnp.float32).astype(jnp.bfloat16)

    def sums(d, k):
        parts = []
        for h in range(2):
            before = block(jnp.maximum(d - 1, 0), h, d > 0 if first and k == 0 else None)
            after = block(jnp.minimum(d + 1, planes - 1), h, d < planes - 1 if not first and k == UNROLL - 1 else None)
            rhs = jnp.concatenate([before, block(d, h, None), after], axis=0)
            terms = jnp.dot(mat_ref[h], rhs, preferred_element_type=jnp.float32)
            parts.append(joined_columns(terms, outs) * inv)
        upper, lower = parts
        return jnp.concatenate(
            [upper[: (half - 1) * outs], upper[(half - 1) * outs :] + lower[: 2 * outs], lower[2 * outs :]]
        )

    def finish(d, whole, flat):
        at = pl.multiple_of(d * outs, outs)
        whole = jnp.concatenate(
            [
                whole[:outs] + above_ref[pl.ds(at, outs), :].astype(jnp.float32),
                whole[outs:-outs],
                whole[-outs:] + below_ref[pl.ds(at, outs), :].astype(jnp.float32),
            ]
        )
        for lane in range(cols // LANES):
            lanes = slice(lane * LANES, (lane + 1) * LANES)
            flat[lane] = whole[:, lanes]
            for o in range(outs):
                out_ref[d, o, :, lanes] = (flat[lane, pl.ds(o, rows, stride=outs), :] + bias_ref[0, o]).astype(jnp.bfloat16)

    def step(i, _):
        for k in range(UNROLL):
            at = i * UNROLL + k
            whole = sums(start + at, k)
            if first:
                out_ref[at] = whole
            else:
                finish(at, early_ref[at], flats[2 * k])
                finish(start + at, whole, flats[2 * k + 1])
        return 0

    lax.fori_loop(0, count // UNROLL, step, 0)


def filtered(inv, bias, variances, mat, rows, outs, early=None, above=None, below=None):
    planes, _, _, cols = variances[0].shape
    vmem = pl.BlockSpec(memory_space=pltpu.VMEM)
    smem = pl.BlockSpec(memory_space=pltpu.SMEM)
    count = planes // 2
    first = early is None
    more = [] if first else [early, above, below]

    def kernel(*refs):
        filter_kernel(planes, 0 if first else count, count, rows, outs, cols, len(variances), *refs)

    return pl.pallas_call(
        kernel,
        out_shape=jax.ShapeDtypeStruct((count, rows * outs, cols), jnp.float32)
        if first
        else jax.ShapeDtypeStruct((planes, outs, rows, cols), jnp.bfloat16),
        in_specs=[smem, smem] + [vmem] * (len(variances) + 1 + len(more)),
        out_specs=vmem,
        scratch_shapes=[]
        if first
        else [pltpu.VMEM((cols // LANES, rows * outs, LANES), jnp.float32)] * (2 * UNROLL),
        compiler_params=pltpu.CompilerParams(vmem_limit_bytes=20 * MIB),
        cost_estimate=pl.CostEstimate(
            flops=2 * count * 2 * mat.shape[1] * mat.shape[2] * cols, bytes_accessed=8 << 20, transcendentals=0
        ),
        name="filter",
    )(inv, bias, *variances, mat, *more)


def matrix_kernel(chunks, group, weight_ref, filter_ref, edge_ref):
    taps, each, chans = weight_ref.shape
    half = filter_ref.shape[1] // each - 1
    width = chans * half
    weight = weight_ref[...].reshape(taps * each, chans)
    chan = lax.broadcasted_iota(jnp.int32, (chans, width), 0)
    lane = lax.broadcasted_iota(jnp.int32, (chans, width), 1)

    def spread(mask):
        onehot = jnp.where(mask, 1.0, 0.0).astype(jnp.bfloat16)
        return jnp.dot(weight, onehot, preferred_element_type=jnp.float32).reshape(taps, each, width)

    by_row = [spread(lane == chan * half + r) for r in range(half)]
    for h in range(2):
        for a in range(3):
            rows = []
            for g in range(half + 1):
                row = jnp.zeros((each, width), jnp.float32)
                for b in range(3):
                    r = g - h + b - 1
                    if 0 <= r < half:
                        row = row + by_row[r][3 * a + b]
                rows.append(row)
            filter_ref[h, :, a * width : (a + 1) * width] = jnp.concatenate(rows).astype(jnp.bfloat16)
    by_plane = []
    for q in range(group):
        mask = chan < 0
        offset = 0
        for size in chunks:
            here = (chan >= offset) & (chan < offset + size)
            mask = mask | (here & (lane == chan + offset * (group - 1) + q * size))
            offset += size
        by_plane.append(spread(mask))
    for side, b in ((0, 2), (1, 0)):
        rows = []
        for p in range(group + 2):
            row = jnp.zeros((each, width), jnp.float32)
            for a in range(3):
                q = a + p - 2
                if 0 <= q < group:
                    row = row + by_plane[q][3 * a + b]
            rows.append(row)
        edge_ref[side] = jnp.concatenate(rows).astype(jnp.bfloat16)


def matrices(weight, rows, chunks, group):
    outs, chans = weight.shape[3:]
    each = 3 * outs
    half = rows // 2
    vmem = pl.BlockSpec(memory_space=pltpu.VMEM)

    def kernel(*refs):
        matrix_kernel(chunks, group, *refs)

    return pl.pallas_call(
        kernel,
        out_shape=(
            jax.ShapeDtypeStruct((2, (half + 1) * each, 3 * chans * half), jnp.bfloat16),
            jax.ShapeDtypeStruct((2, (group + 2) * each, group * chans), jnp.bfloat16),
        ),
        in_specs=[vmem],
        out_specs=(vmem, vmem),
        compiler_params=pltpu.CompilerParams(vmem_limit_bytes=16 * MIB),
        name="matrices",
    )(weight.reshape(9, each, chans))


def on_device(
    ref_feat, src_feat, row_tap, row_frac, col_tap, col_frac, view_count, conv_weight, conv_bias
):
    rows = ref_feat.shape[1]
    outs = conv_weight.shape[3]
    tile = lax.axis_index("tile")

    inv = (1.0 / (1.0 + view_count.astype(jnp.float32))).reshape(1, 1)
    rowmat, colmat = tables(tile, view_count, row_tap, row_frac, col_tap, col_frac)

    sizes = [size for chunk in PARTS for size in chunk]
    pieces = [src_feat[:, sum(sizes[:i]) : sum(sizes[: i + 1])] for i in range(len(sizes))]
    pieces[1:] = lax.optimization_barrier(pieces[1:])
    across = [routed(piece, lambda i: i ^ 2) for piece in pieces]
    beside = [routed(piece, lambda i: i ^ 1) for piece in pieces]
    across[0], rowmat, colmat, ref_feat, conv_weight = lax.optimization_barrier(
        (across[0], rowmat, colmat, ref_feat, conv_weight)
    )
    along = [routed(across[0], onward)]
    base = ref_feat.astype(jnp.float32)
    bases = [base[sum(CHUNKS[:i]) : sum(CHUNKS[: i + 1])] for i in range(len(CHUNKS))]
    filter_mat, edge_mat = matrices(conv_weight, rows, CHUNKS, GROUP)
    variances = []
    edges = []
    begin = 0
    across_beside = []
    for i, chunk in enumerate(PARTS):
        end = begin + len(chunk)
        ahead = end + (len(PARTS[i + 1]) if i + 1 < len(PARTS) else 0)
        along += [routed(part, onward) for part in across[len(along) : ahead]]
        across_beside += [routed(part, lambda i: i ^ 1) for part in across[len(across_beside) : ahead]]
        here = slice(begin, end)
        along_beside = [routed(part, lambda i: i ^ 1) for part in along[here]]
        strips = [pieces[here], beside[here], across[here], across_beside[here], along[here], along_beside]
        var, edge = warp(inv, strips, bases[i], rowmat, colmat)
        if i + 1 < len(PARTS):
            var, edge, along[end:], across_beside[end:], across[ahead:] = lax.optimization_barrier(
                (var, edge, along[end:], across_beside[end:], across[ahead:])
            )
        variances.append(var)
        edges.append(edge)
        begin = end
    up, down = edge_terms(inv, edges, edge_mat, outs)
    above = routed(down, lambda i: i + 1)
    below = routed(up, lambda i: i - 1)
    bias = conv_bias.reshape(1, -1)
    early = filtered(inv, bias, variances, filter_mat, rows, outs)
    return filtered(inv, bias, variances, filter_mat, rows, outs, early, above, below)


def solution(mesh):
    placed = (
        P("groups", "tile", None),
        P("groups", None, "tile", None),
        P("groups", None, "tile"),
        P("groups", None, "tile"),
        P("groups", None, None),
        P("groups", None, None),
        P(("groups", "tile")),
        P(),
        P(),
    )
    return jax.shard_map(
        on_device,
        mesh=mesh,
        in_specs=placed,
        out_specs=P("groups", None, "tile", None),
        check_vma=False,
    )
```
